32 devices in a mesh: dp: 4 (over z), blk: 2 (over x), uly: 4 (over y, core).
Axes of the slice: x: 2, y: 2, z: 4, core: 2. Of those that a mesh axis runs over, the one named last changes fastest.
Arguments:
- tokens: bfloat16 [4096, 1536], P(('dp', 'blk', 'uly')), may hold values from -6 to 6
- routes: int32 [4096, 8], P(('dp', 'blk', 'uly')), may hold values from 0 to 39, all different within a row; in each aligned block of 128 rows (0 to 127, 128 to 255, ...) at most 32 rows name the same one
- gates: float32 [4096, 8], P(('dp', 'blk', 'uly')), may hold values from 0.05 to 0.25
- qkv_weight: bfloat16 [1536, 2560], P(('dp', 'blk', 'uly')), may hold values from -0.21875 to 0.21875
- out_weight: bfloat16 [1536, 1536], P(('dp', 'blk', 'uly')), may hold values from -1.75 to 1.75
- attn_gain: bfloat16 [1536], P(('dp', 'blk', 'uly')), may hold values from 0.5 to 1.5
- moe_gain: bfloat16 [1536], P(('dp', 'blk', 'uly')), may hold values from 0.5 to 1.5
- expert_in: bfloat16 [40, 1536, 1024], P('uly', ('dp', 'blk')), may hold values from -0.15625 to 0.15625
- expert_out: bfloat16 [40, 512, 1536], P('uly', ('dp', 'blk')), may hold values from -1 to 1
- cotangent: float32 [4096, 1536], P(('dp', 'blk', 'uly')), may hold values from -6 to 6
Outputs:
- mixed: float32 [4096, 1536], P(('dp', 'blk', 'uly'))
- tokens_grad: float32 [4096, 1536], P(('dp', 'blk', 'uly'))
- qkv_grad: float32 [1536, 2560], P(('dp', 'blk', 'uly'))
- out_grad: float32 [1536, 1536], P(('dp', 'blk', 'uly'))
- attn_gain_grad: float32 [1536], P(('dp', 'blk', 'uly'))
- moe_gain_grad: float32 [1536], P(('dp', 'blk', 'uly'))
- expert_in_grad: float32 [40, 1536, 1024], P('uly', ('dp', 'blk'))
- expert_out_grad: float32 [40, 512, 1536], P('uly', ('dp', 'blk'))
The draws below stay inside these ranges and needn't reach their ends.
Inputs may be any that keep to these rules, and one draw needn't show every extreme that they name: `routes`: each row names 8 different experts; among the 128 rows of one device no expert is named by more than 32 rows, a bound that some block reaches.
All inputs are finite; a program needn't handle non-finite values.
Results may differ from the reference program's by a relative error of at most 0.017.
Values may be sent and summed in bfloat16 or wider, within the bound.
A program may use at most 320 MiB of HBM per device.

```python
import math
import jax
import jax.numpy as jnp
import numpy as np
from jax import lax

D = 1536
QUERY_HEADS = 24
KEY_VALUE_HEADS = 8
HEAD_DIMENSION = 64
E = 40
F = 512
TOPK = 8
TOK_DEV = 128
CAP = 32
SEQUENCE_TOKENS = 1024
SEQS = 4
TOKENS = 4096
QKV = 2560


def block_scale(own_key, dims, shards, low, largest):
    factor_of = 1.0
    for axis_at, parts in shards:
        heights = jax.random.uniform(jax.random.fold_in(jax.random.fold_in(own_key, 6), axis_at), (parts,), jnp.float32, low / len(shards), largest / len(shards))
        factor_of = factor_of * jnp.repeat(jnp.exp(heights), dims[axis_at] // parts).reshape((-1,) + (1,) * (len(dims) - 1 - axis_at))
    return factor_of


def routed_block(own_key, own, number, rows, amount, top, limit, skew):
    order = jax.random.permutation(own_key, amount)
    heavy_load, common = shares(amount, rows * top, limit, skew, True), shares(amount, rows * top, limit, skew, False)
    places = jnp.arange(amount)

    def named(sizes, offset_by):
        used = int((sizes > 0).sum())
        fixed = max(1, used // 4)
        moved = fixed + (places - fixed + offset_by * (used - fixed)) % max(1, amount - fixed)
        return jnp.zeros((amount,), jnp.int32).at[order[jnp.where(places < fixed, places, moved)]].set(jnp.asarray(sizes, jnp.int32))

    sizes = jnp.where(number % 4 == 0, named(heavy_load, number // 4), named(common, number - number // 4 - 1))
    mixed = jax.random.permutation(jax.random.fold_in(own, 3), amount)
    donor, sink = mixed[0:amount // 2 * 2:2], mixed[1:amount // 2 * 2:2]
    room = jnp.minimum(sizes[donor] - 1, limit - sizes[sink]) // 2
    room = jnp.where((donor == order[0]) | (sink == order[0]) | (sizes[sink] == 0), 0, jnp.maximum(room, 0))
    moved = jax.random.randint(jax.random.fold_in(own, 4), (amount // 2,), 0, 1 << 20) % (room + 1)
    sizes = sizes.at[donor].add(-moved).at[sink].add(moved)
    members = jnp.searchsorted(jnp.cumsum(sizes), jnp.arange(rows * top), side="right").astype(jnp.int32)
    listing = members.reshape(top, rows).T
    listing = listing[jax.random.permutation(jax.random.fold_in(own, 1), rows)]
    offset_by = jax.random.randint(jax.random.fold_in(own, 2), (rows, 1), 0, top)
    return jnp.take_along_axis(listing, (jnp.arange(top)[None, :] + offset_by) % top, axis=1)


def shares(number_of, total, limit, slope, full):
    loads = [(1 << 20) // math.isqrt(rank ** slope) + 1 for rank in range(1, number_of + 1)]
    largest = limit if full else min(limit, max(-(-total // number_of), total * loads[0] // sum(loads)))
    least = 1 if total - largest >= number_of - 1 else 0
    given, surplus = [largest] + [least] * (number_of - 1), total - largest - least * (number_of - 1)
    while surplus > 0:
        movable = [i for i in range(1, number_of) if given[i] < largest] or [i for i in range(1, number_of) if given[i] < limit]
        whole, remaining = sum([loads[i] for i in movable]), surplus
        for i in movable:
            extra = min(limit - given[i], max(1, remaining * loads[i] // whole), surplus)
            given[i] = given[i] + extra
            surplus = surplus - extra
    return np.array(given)


def noise(key, shape, scale, reach, cuts=(), held_as=jnp.bfloat16):
    loudness = block_scale(key, shape, cuts, -0.22, 0.18) if cuts else 1.0
    drawn = jax.random.normal(key, shape, jnp.float32) * scale * loudness
    return jnp.minimum(jnp.maximum(drawn, -reach), reach).astype(held_as)


def setup_inputs(seed: int = 0) -> dict:
    keys = jax.random.split(jax.random.key(seed), 11)
    tokens = noise(keys[0], (TOKENS, D), 1.0, 6.0, ((0, 32),))
    routes_keys = jax.random.split(jax.random.fold_in(keys[1], 1), TOKENS // TOK_DEV)
    routes_turns = jax.random.permutation(jax.random.fold_in(keys[1], 3), TOKENS // TOK_DEV)
    routes = jax.vmap(lambda own, number: routed_block(jax.random.fold_in(keys[1], 2), own, number, TOK_DEV, E, TOPK, CAP, 1))(routes_keys, routes_turns).reshape((TOKENS, TOPK))
    gates = jnp.clip(jnp.exp(math.log(0.25) - 1.609438 * jax.random.uniform(keys[2], (TOKENS, TOPK), jnp.float32) ** block_scale(keys[2], (TOKENS, TOPK), ((0, 32),), -0.2, 0.2)), 0.05, 0.25)
    qkv_weight = noise(keys[3], (D, QKV), (D // 2) ** -0.5, 0.21875, ((0, 32),))
    out_weight = noise(keys[4], (QUERY_HEADS * HEAD_DIMENSION, D), (max(1, D // 128)) ** -0.5, 1.75, ((0, 32),))
    attn_gain = jnp.clip(1.0 + 0.1 * jax.random.normal(keys[5], (D,), jnp.float32), 0.5, 1.5).astype(jnp.bfloat16)
    moe_gain = jnp.clip(1.0 + 0.1 * jax.random.normal(keys[6], (D,), jnp.float32), 0.5, 1.5).astype(jnp.bfloat16)
    expert_in = noise(keys[7], (E, D, 2 * F), D ** -0.5, 0.15625, ((0, 4), (1, 8)))
    expert_out = noise(keys[8], (E, F, D), (max(1, F // 16)) ** -0.5, 1.0, ((0, 4), (1, 8)))
    cotangent = noise(keys[9], (TOKENS, D), 1.0, 6.0, ((0, 32),), jnp.float32)
    return dict(tokens=tokens, routes=routes, gates=gates, qkv_weight=qkv_weight, out_weight=out_weight, attn_gain=attn_gain, moe_gain=moe_gain, expert_in=expert_in, expert_out=expert_out, cotangent=cotangent)


@jax.custom_vjp
def reduced_precision(v):
    return lax.optimization_barrier(v.astype(jnp.bfloat16)).astype(jnp.float32)

@jax.custom_vjp
def reduced_precision_backward(v):
    return v

def low_keep(v):
    return (reduced_precision(v), None)

def low_pass(kept, grad):
    return (grad,)

def back_keep(v):
    return (v, None)

def back_low(kept, grad):
    return (reduced_precision(grad),)
reduced_precision.defvjp(low_keep, low_pass)
reduced_precision_backward.defvjp(back_keep, back_low)
norm_eps = 1e-06
masked_score = -1e+30
highest = lax.Precision.HIGHEST

def matmul(left, right):
    return jnp.dot(left, right, precision=highest)

def normalize(values, gain):
    return values * lax.rsqrt(lax.optimization_barrier(jnp.mean(values * values, axis=-1, keepdims=True)) + norm_eps) * gain

def apply_rotation(values, token_positions):
    half_size = values.shape[-1] // 2
    frequency = 10000.0 ** (-(jnp.arange(half_size, dtype=jnp.float32) * 2.0 / values.shape[-1]))
    angles = token_positions[:, None] * frequency[None, :]
    cosine_table = jnp.cos(angles)[:, None, :]
    sine_portion = jnp.sin(angles)[:, None, :]
    first_half = values[..., :half_size]
    second = values[..., half_size:]
    return jnp.concatenate([first_half * cosine_table - second * sine_portion, second * cosine_table + first_half * sine_portion], axis=-1)

def route_slots(block_routes):
    expert_ids = jnp.arange(E, dtype=jnp.int32)
    onehot = (block_routes[:, :, None] == expert_ids[None, None, :]).astype(jnp.int32).reshape(-1, E)
    before = jnp.cumsum(onehot, axis=0) - onehot
    return lax.optimization_barrier(jnp.sum(before * onehot, axis=1)).reshape(block_routes.shape).astype(jnp.int32)

def attention(queries, keys_in, values_in):
    query_group_size = QUERY_HEADS // KEY_VALUE_HEADS
    keys_all = jnp.repeat(keys_in, query_group_size, axis=1)
    values_all = jnp.repeat(values_in, query_group_size, axis=1)
    block_size = min(512, SEQUENCE_TOKENS)
    starts = jnp.arange(SEQUENCE_TOKENS // block_size, dtype=jnp.int32) * block_size
    score_scale = HEAD_DIMENSION ** (-0.5)
    key_positions = jnp.arange(SEQUENCE_TOKENS, dtype=jnp.int32)

    @jax.checkpoint
    def one_block(first_row):
        query_block = lax.dynamic_slice_in_dim(queries, first_row, block_size, 0)
        scores = jnp.einsum('qhd,khd->hqk', query_block, keys_all, precision=highest) * score_scale
        scores = reduced_precision_backward(scores)
        query_positions = first_row + jnp.arange(block_size, dtype=jnp.int32)
        visible = key_positions[None, None, :] <= query_positions[None, :, None]
        scores = jnp.where(visible, scores, masked_score)
        probs = reduced_precision(jax.nn.softmax(scores, axis=-1))
        return jnp.einsum('hqk,khd->qhd', probs, values_all, precision=highest)
    outputs = lax.map(one_block, starts)
    return outputs.reshape(SEQUENCE_TOKENS, QUERY_HEADS, HEAD_DIMENSION)

def experts(normed_two, seq_routes, seq_gates, w_in, w_out):
    blocks = SEQUENCE_TOKENS // TOK_DEV
    block_routes = seq_routes.reshape(blocks, TOK_DEV, TOPK)
    slots = jax.vmap(route_slots)(block_routes)
    block_ids = jnp.broadcast_to(jnp.arange(blocks, dtype=jnp.int32)[:, None, None], block_routes.shape)
    token_ids = jnp.broadcast_to(jnp.arange(blocks, dtype=jnp.int32)[:, None, None] * TOK_DEV + jnp.arange(TOK_DEV, dtype=jnp.int32)[None, :, None], block_routes.shape)
    slot_table = jnp.full((E, blocks, CAP), SEQUENCE_TOKENS, jnp.int32).at[block_routes, block_ids, slots].set(token_ids)
    gate_table = jnp.zeros((E, blocks, CAP), jnp.float32).at[block_routes, block_ids, slots].set(seq_gates.reshape(blocks, TOK_DEV, TOPK))
    slot_table = slot_table.reshape(E, blocks * CAP)
    padded = jnp.concatenate([normed_two, jnp.zeros((1, D), jnp.float32)], axis=0)
    routed_rows = reduced_precision_backward(padded[slot_table])
    gate_up = reduced_precision_backward(jnp.einsum('erd,edf->erf', routed_rows, w_in, precision=highest))
    activated = reduced_precision(jax.nn.silu(gate_up[..., :F]) * gate_up[..., F:])
    expert_result = reduced_precision(reduced_precision_backward(jnp.einsum('erf,efd->erd', activated, w_out, precision=highest)))
    weighted = gate_table.reshape(E, blocks * CAP)[..., None] * expert_result
    combined = jnp.zeros((SEQUENCE_TOKENS + 1, D), jnp.float32).at[slot_table.reshape(-1)].add(weighted.reshape(-1, D))
    return combined[:SEQUENCE_TOKENS]

def sequence_layer(inputs, seq_routes, seq_gates, qkv_w, out_w, gain_attn, gain_moe, w_in, w_out):
    normed_one = reduced_precision(normalize(inputs, gain_attn))
    projected_rows = reduced_precision_backward(matmul(normed_one, qkv_w))
    query_portion = QUERY_HEADS * HEAD_DIMENSION
    key_portion = KEY_VALUE_HEADS * HEAD_DIMENSION
    token_positions = jnp.arange(SEQUENCE_TOKENS, dtype=jnp.float32)
    queries = reduced_precision_backward(reduced_precision(apply_rotation(projected_rows[:, :query_portion].reshape(SEQUENCE_TOKENS, QUERY_HEADS, HEAD_DIMENSION), token_positions)))
    sequence_keys = reduced_precision_backward(reduced_precision(apply_rotation(projected_rows[:, query_portion:query_portion + key_portion].reshape(SEQUENCE_TOKENS, KEY_VALUE_HEADS, HEAD_DIMENSION), token_positions)))
    sequence_values = reduced_precision_backward(reduced_precision(projected_rows[:, query_portion + key_portion:].reshape(SEQUENCE_TOKENS, KEY_VALUE_HEADS, HEAD_DIMENSION)))
    head_out = reduced_precision_backward(reduced_precision(attention(queries, sequence_keys, sequence_values).reshape(SEQUENCE_TOKENS, query_portion)))
    attention_out = reduced_precision_backward(matmul(head_out, out_w))
    hidden = inputs + attention_out
    normed_two = reduced_precision(normalize(hidden, gain_moe))
    return hidden + experts(normed_two, seq_routes, seq_gates, w_in, w_out)

def reference(tokens, routes, gates, qkv_weight, out_weight, attn_gain, moe_gain, expert_in, expert_out, cotangent):

    def forward(inputs, qkv_w, out_w, gain_attn, gain_moe, w_in, w_out):

        def run_one(sequence_item):
            return sequence_layer(sequence_item[0], sequence_item[1], sequence_item[2], qkv_w, out_w, gain_attn, gain_moe, w_in, w_out)
        outputs = lax.map(jax.checkpoint(run_one), (inputs.reshape(SEQS, SEQUENCE_TOKENS, D), routes.reshape(SEQS, SEQUENCE_TOKENS, TOPK), gates.reshape(SEQS, SEQUENCE_TOKENS, TOPK)))
        return outputs.reshape(TOKENS, D)
    mixed, pullback = jax.vjp(forward, tokens.astype(jnp.float32), qkv_weight.astype(jnp.float32), out_weight.astype(jnp.float32), attn_gain.astype(jnp.float32), moe_gain.astype(jnp.float32), expert_in.astype(jnp.float32), expert_out.astype(jnp.float32))
    grads = pullback(cotangent)
    return (mixed, grads[0], grads[1], grads[2], grads[3], grads[4], grads[5], grads[6])
```

```python
import jax
import jax.numpy as jnp
from jax import lax
from jax.sharding import PartitionSpec as P

QUERY_HEADS = 24
KEY_VALUE_HEADS = 8
HEAD_DIMENSION = 64
E = 40
F = 512


norm_eps = 1e-06
masked_score = -1e30


def passed_along(value, axis, steps):
    count = lax.axis_size(axis)
    leading, last = (max(0, -steps), min(count, count - steps))
    return lax.ppermute(value, axis, [(source, source + steps) for source in range(leading, last)])


def rope_tables(token_positions, head_size):
    half_size = head_size // 2
    frequency = 10000.0 ** (-(jnp.arange(half_size, dtype=jnp.float32) * 2.0 / head_size))
    angles = token_positions.astype(jnp.float32)[:, None] * frequency[None, :]
    return (jnp.cos(angles)[:, None, :], jnp.sin(angles)[:, None, :])


def apply_rotation(values, cosine_table, sine_portion):
    half_size = values.shape[-1] // 2
    first_half = values[..., :half_size]
    second = values[..., half_size:]
    return jnp.concatenate(
        [
            first_half * cosine_table - second * sine_portion,
            second * cosine_table + first_half * sine_portion,
        ],
        axis=-1,
    )


def unrotate(grads, cosine_table, sine_portion):
    half_size = grads.shape[-1] // 2
    first_half = grads[..., :half_size]
    second = grads[..., half_size:]
    return jnp.concatenate(
        [
            first_half * cosine_table + second * sine_portion,
            second * cosine_table - first_half * sine_portion,
        ],
        axis=-1,
    )


def normalize_parts(values):
    inverse = lax.rsqrt(jnp.mean(values * values, axis=-1, keepdims=True) + norm_eps)
    return (values * inverse, inverse)


def norm_back(grad_out, scaled, inverse, gain):
    grad_scaled = grad_out * gain
    grad_gain = jnp.sum(grad_out * scaled, axis=0)
    grad_values = inverse * (
        grad_scaled - scaled * jnp.mean(grad_scaled * scaled, axis=-1, keepdims=True)
    )
    return (grad_values, grad_gain)


def shards(
    tokens,
    routes,
    gates,
    qkv_weight,
    out_weight,
    attn_gain,
    moe_gain,
    expert_in,
    expert_out,
    cotangent,
):
    local_row_count = tokens.shape[0]
    width = tokens.shape[1]
    sequence_split_count = lax.axis_size("uly")
    blk_index = lax.axis_index("blk")
    uly_index = lax.axis_index("uly")
    q_heads = QUERY_HEADS // sequence_split_count
    key_value_heads = KEY_VALUE_HEADS // sequence_split_count
    query_group_size = QUERY_HEADS // KEY_VALUE_HEADS
    q_width = q_heads * HEAD_DIMENSION
    kv_width = key_value_heads * HEAD_DIMENSION
    seq_rows = local_row_count * sequence_split_count
    block_size = min(512, seq_rows)
    block_count = seq_rows // block_size
    score_scale = HEAD_DIMENSION ** (-0.5)
    local_experts = E // sequence_split_count
    query_portion = QUERY_HEADS * HEAD_DIMENSION
    key_portion = KEY_VALUE_HEADS * HEAD_DIMENSION
    qkv_full, out_full, gain_attn, gain_moe = (
        lax.all_gather(qkv_weight, ("dp", "blk", "uly"), axis=0, tiled=True),
        lax.all_gather(out_weight, ("dp", "blk", "uly"), axis=0, tiled=True),
        lax.all_gather(attn_gain, ("dp", "blk", "uly"), axis=0, tiled=True),
        lax.all_gather(moe_gain, ("dp", "blk", "uly"), axis=0, tiled=True),
    )
    slice_count = lax.axis_size("dp") * lax.axis_size("blk")
    hidden_slice = F // slice_count
    hidden_columns = local_experts * hidden_slice
    w_out = expert_out.reshape(hidden_columns, width)
    w_in = lax.all_to_all(
        expert_in.reshape(local_experts, width // slice_count, 2, slice_count, hidden_slice)
        .transpose(3, 1, 2, 0, 4)
        .reshape(slice_count, width // slice_count, 2 * hidden_columns),
        ("dp", "blk"),
        split_axis=0,
        concat_axis=0,
        tiled=True,
    ).reshape(width, 2 * hidden_columns)
    all_cotangent = lax.all_gather(
        cotangent.astype(jnp.bfloat16), ("dp", "blk", "uly"), axis=0, tiled=True
    )
    gain_attn = gain_attn.astype(jnp.float32)
    gain_moe = gain_moe.astype(jnp.float32)
    inputs = tokens.astype(jnp.float32)
    scaled_one, inverse_one = normalize_parts(inputs)
    normed_one = (scaled_one * gain_attn).astype(jnp.bfloat16)
    projected_rows = jnp.dot(normed_one, qkv_full, preferred_element_type=jnp.float32)
    token_positions = (blk_index * sequence_split_count + uly_index) * local_row_count + jnp.arange(
        local_row_count, dtype=jnp.int32
    )
    cosine_table, sine_portion = rope_tables(token_positions, HEAD_DIMENSION)
    queries = apply_rotation(
        projected_rows[:, :query_portion].reshape(local_row_count, QUERY_HEADS, HEAD_DIMENSION),
        cosine_table,
        sine_portion,
    )
    sequence_keys = apply_rotation(
        projected_rows[:, query_portion : query_portion + key_portion].reshape(
            local_row_count, KEY_VALUE_HEADS, HEAD_DIMENSION
        ),
        cosine_table,
        sine_portion,
    )
    sequence_values = projected_rows[:, query_portion + key_portion :]
    packed = jnp.concatenate(
        [
            queries.reshape(local_row_count, sequence_split_count, q_width),
            sequence_keys.reshape(local_row_count, sequence_split_count, kv_width),
            sequence_values.reshape(local_row_count, sequence_split_count, kv_width),
        ],
        axis=2,
    ).astype(jnp.bfloat16)
    by_heads = lax.all_to_all(packed, "uly", split_axis=1, concat_axis=0, tiled=True).reshape(
        seq_rows, q_width + 2 * kv_width
    )
    local_queries = by_heads[:, :q_width]
    kv_own = by_heads[:, q_width:]
    kv_prev = passed_along(kv_own, "blk", 1)
    kv_all = jnp.concatenate([kv_prev, kv_own], axis=0)
    key_rows = kv_all[:, :kv_width].reshape(2 * seq_rows, key_value_heads, HEAD_DIMENSION)
    value_rows = kv_all[:, kv_width:].reshape(2 * seq_rows, key_value_heads, HEAD_DIMENSION)
    query_base = blk_index * seq_rows
    key_positions = (blk_index - 1) * seq_rows + jnp.arange(2 * seq_rows, dtype=jnp.int32)

    def block_scores(first_row):
        query_block = lax.dynamic_slice_in_dim(local_queries, first_row, block_size, 0).reshape(
            block_size, key_value_heads, query_group_size, HEAD_DIMENSION
        )
        scores = (
            jnp.einsum("qkgd,skd->kgqs", query_block, key_rows, preferred_element_type=jnp.float32)
            * score_scale
        )
        query_positions = query_base + first_row + jnp.arange(block_size, dtype=jnp.int32)
        visible = (key_positions[None, :] <= query_positions[:, None]) & (
            key_positions[None, :] >= 0
        )
        return (query_block, jnp.where(visible, scores, masked_score))

    def attend(block_index):
        query_block, scores = block_scores(block_index * block_size)
        row_max = jnp.max(scores, axis=-1, keepdims=True)
        weights = jnp.exp(scores - row_max)
        weight_sum = jnp.sum(weights, axis=-1, keepdims=True)
        probs = (weights / weight_sum).astype(jnp.bfloat16)
        mixed_block = jnp.einsum(
            "kgqs,skd->qkgd", probs, value_rows, preferred_element_type=jnp.float32
        )
        return (
            mixed_block.reshape(block_size, q_width).astype(jnp.bfloat16),
            (row_max + jnp.log(weight_sum))[..., 0],
        )

    head_out, log_sums = lax.map(attend, jnp.arange(block_count, dtype=jnp.int32))
    head_out = head_out.reshape(seq_rows, 1, q_width)
    seq_out = lax.all_to_all(head_out, "uly", split_axis=0, concat_axis=1, tiled=True).reshape(
        local_row_count, query_portion
    )
    attention_out = jnp.dot(seq_out, out_full, preferred_element_type=jnp.float32)
    hidden = inputs + attention_out
    scaled_two, inverse_two = normalize_parts(hidden)
    normed_two = (scaled_two * gain_moe).astype(jnp.bfloat16)
    all_axes = ("dp", "blk", "uly")
    expert_ids = uly_index * local_experts + jnp.arange(local_experts, dtype=jnp.int32)
    all_routes = lax.all_gather(routes, all_axes, axis=0, tiled=True)
    all_gates = lax.all_gather(gates, all_axes, axis=0, tiled=True)
    gate_table = jnp.sum(
        jnp.where(all_routes[:, :, None] == expert_ids[None, None, :], all_gates[:, :, None], 0.0),
        axis=1,
    )
    gate_table = jnp.broadcast_to(
        gate_table[:, :, None], (gate_table.shape[0], local_experts, hidden_slice)
    ).reshape(gate_table.shape[0], hidden_columns)
    all_rows = lax.all_gather(normed_two, all_axes, axis=0, tiled=True)
    gate_up = jnp.dot(all_rows, w_in, preferred_element_type=jnp.float32)
    gate_part = gate_up[:, :hidden_columns]
    up_part = gate_up[:, hidden_columns:]
    sigmoid_gate = jax.nn.sigmoid(gate_part)
    silu_gate = gate_part * sigmoid_gate
    activated = (silu_gate * up_part * gate_table).astype(jnp.bfloat16)
    mixed_part = jnp.dot(activated, w_out, preferred_element_type=jnp.float32)
    grad_act = (
        jnp.dot(all_cotangent, w_out.T, preferred_element_type=jnp.float32) * gate_table
    )
    grad_gate = grad_act * up_part * sigmoid_gate * (1.0 + gate_part * (1.0 - sigmoid_gate))
    grad_up = grad_act * silu_gate
    grad_gate_up = jnp.concatenate([grad_gate, grad_up], axis=-1).astype(jnp.bfloat16)
    rows_part = jnp.dot(grad_gate_up, w_in.T, preferred_element_type=jnp.float32)
    grad_normed_two = lax.psum_scatter(
        rows_part.astype(jnp.bfloat16), all_axes, scatter_dimension=0, tiled=True
    ).astype(jnp.float32)
    mixed = hidden + lax.psum_scatter(
        mixed_part.astype(jnp.bfloat16), all_axes, scatter_dimension=0, tiled=True
    ).astype(jnp.float32)
    grad_w_out = jnp.dot(activated.T, all_cotangent, preferred_element_type=jnp.float32)
    grad_w_in = jnp.dot(all_rows.T, grad_gate_up, preferred_element_type=jnp.float32)
    grad_out_shard = grad_w_out.reshape(local_experts, hidden_slice, width)
    grad_in_shard = (
        lax.all_to_all(
            grad_w_in.astype(jnp.bfloat16).reshape(slice_count, width // slice_count, 2 * hidden_columns),
            ("dp", "blk"),
            split_axis=0,
            concat_axis=0,
            tiled=True,
        )
        .reshape(slice_count, width // slice_count, 2, local_experts, hidden_slice)
        .transpose(3, 1, 2, 0, 4)
        .reshape(local_experts, width // slice_count, 2 * F)
        .astype(jnp.float32)
    )
    grad_hidden_norm, grad_gain_moe = norm_back(grad_normed_two, scaled_two, inverse_two, gain_moe)
    grad_hidden = cotangent + grad_hidden_norm
    hidden_low = grad_hidden.astype(jnp.bfloat16)
    grad_out_weight = jnp.dot(seq_out.T, hidden_low, preferred_element_type=jnp.float32)
    grad_seq_out = jnp.dot(hidden_low, out_full.T, preferred_element_type=jnp.float32).astype(
        jnp.bfloat16
    )
    grad_heads = lax.all_to_all(
        grad_seq_out.reshape(local_row_count, sequence_split_count, q_width),
        "uly",
        split_axis=1,
        concat_axis=0,
        tiled=True,
    ).reshape(seq_rows, q_width)

    def attend_back(carry, block_index):
        grad_keys, grad_values = carry
        first_row = block_index * block_size
        query_block, scores = block_scores(first_row)
        probs = jnp.exp(scores - log_sums[block_index][..., None])
        probs_low = probs.astype(jnp.bfloat16)
        grad_block = lax.dynamic_slice_in_dim(grad_heads, first_row, block_size, 0).reshape(
            block_size, key_value_heads, query_group_size, HEAD_DIMENSION
        )
        grad_values = grad_values + jnp.einsum(
            "kgqs,qkgd->skd", probs_low, grad_block, preferred_element_type=jnp.float32
        )
        grad_probs = jnp.einsum(
            "qkgd,skd->kgqs", grad_block, value_rows, preferred_element_type=jnp.float32
        )
        centre = jnp.sum(probs * grad_probs, axis=-1, keepdims=True)
        grad_scores = (probs * (grad_probs - centre)).astype(jnp.bfloat16)
        grad_query = (
            jnp.einsum("kgqs,skd->qkgd", grad_scores, key_rows, preferred_element_type=jnp.float32)
            * score_scale
        )
        grad_keys = (
            grad_keys
            + jnp.einsum(
                "kgqs,qkgd->skd", grad_scores, query_block, preferred_element_type=jnp.float32
            )
            * score_scale
        )
        return ((grad_keys, grad_values), grad_query.reshape(block_size, q_width))

    zero_kv = jnp.zeros((2 * seq_rows, key_value_heads, HEAD_DIMENSION), jnp.float32)
    (grad_keys, grad_values), grad_queries = lax.scan(
        attend_back, (zero_kv, zero_kv), jnp.arange(block_count, dtype=jnp.int32)
    )
    grad_kv = jnp.concatenate(
        [grad_keys.reshape(2 * seq_rows, kv_width), grad_values.reshape(2 * seq_rows, kv_width)],
        axis=1,
    )
    from_next = passed_along(grad_kv[:seq_rows].astype(jnp.bfloat16), "blk", -1).astype(jnp.float32)
    grad_kv_own = grad_kv[seq_rows:] + from_next
    grad_pack = (
        jnp.concatenate([grad_queries.reshape(seq_rows, q_width), grad_kv_own], axis=1)
        .astype(jnp.bfloat16)
        .reshape(seq_rows, 1, q_width + 2 * kv_width)
    )
    grad_seq = lax.all_to_all(grad_pack, "uly", split_axis=0, concat_axis=1, tiled=True)
    grad_q = unrotate(
        grad_seq[:, :, :q_width]
        .astype(jnp.float32)
        .reshape(local_row_count, QUERY_HEADS, HEAD_DIMENSION),
        cosine_table,
        sine_portion,
    )
    grad_k = unrotate(
        grad_seq[:, :, q_width : q_width + kv_width]
        .astype(jnp.float32)
        .reshape(local_row_count, KEY_VALUE_HEADS, HEAD_DIMENSION),
        cosine_table,
        sine_portion,
    )
    grad_v = (
        grad_seq[:, :, q_width + kv_width :]
        .astype(jnp.float32)
        .reshape(local_row_count, key_portion)
    )
    grad_projected = jnp.concatenate(
        [
            grad_q.reshape(local_row_count, query_portion),
            grad_k.reshape(local_row_count, key_portion),
            grad_v,
        ],
        axis=1,
    ).astype(jnp.bfloat16)
    grad_qkv_weight = jnp.dot(normed_one.T, grad_projected, preferred_element_type=jnp.float32)
    grad_normed_one = jnp.dot(grad_projected, qkv_full.T, preferred_element_type=jnp.float32)
    grad_input_norm, grad_gain_attn = norm_back(grad_normed_one, scaled_one, inverse_one, gain_attn)
    grad_tokens = grad_hidden + grad_input_norm
    qkv_shard, out_shard, gain_attn_shard, gain_moe_shard = (
        lax.psum_scatter(grad_qkv_weight.astype(jnp.bfloat16), ("dp", "blk", "uly"), scatter_dimension=0, tiled=True),
        lax.psum_scatter(grad_out_weight.astype(jnp.bfloat16), ("dp", "blk", "uly"), scatter_dimension=0, tiled=True),
        lax.psum_scatter(grad_gain_attn, ("dp", "blk", "uly"), scatter_dimension=0, tiled=True),
        lax.psum_scatter(grad_gain_moe, ("dp", "blk", "uly"), scatter_dimension=0, tiled=True),
    )
    return (
        mixed,
        grad_tokens,
        qkv_shard.astype(jnp.float32),
        out_shard.astype(jnp.float32),
        gain_attn_shard,
        gain_moe_shard,
        grad_in_shard,
        grad_out_shard,
    )


def solution(mesh):
    in_specs = (
        P(("dp", "blk", "uly"), None),
        P(("dp", "blk", "uly"), None),
        P(("dp", "blk", "uly"), None),
        P(("dp", "blk", "uly"), None),
        P(("dp", "blk", "uly"), None),
        P(("dp", "blk", "uly")),
        P(("dp", "blk", "uly")),
        P("uly", ("dp", "blk"), None),
        P("uly", ("dp", "blk"), None),
        P(("dp", "blk", "uly"), None),
    )
    out_specs = (
        P(("dp", "blk", "uly"), None),
        P(("dp", "blk", "uly"), None),
        P(("dp", "blk", "uly"), None),
        P(("dp", "blk", "uly"), None),
        P(("dp", "blk", "uly")),
        P(("dp", "blk", "uly")),
        P("uly", ("dp", "blk"), None),
        P("uly", ("dp", "blk"), None),
    )
    return jax.shard_map(shards, mesh=mesh, in_specs=in_specs, out_specs=out_specs, check_vma=False)
```

```python
import jax
import jax.numpy as jnp
from jax import lax
from jax.sharding import PartitionSpec as P

QUERY_HEADS = 24
KEY_VALUE_HEADS = 8
HEAD_DIMENSION = 64
E = 40
F = 512


norm_eps = 1e-06
masked_score = -1e30


def passed_along(value, axis, steps):
    count = lax.axis_size(axis)
    leading, last = (max(0, -steps), min(count, count - steps))
    return lax.ppermute(value, axis, [(source, source + steps) for source in range(leading, last)])


def rope_tables(token_positions, head_size):
    half_size = head_size // 2
    frequency = 10000.0 ** (-(jnp.arange(half_size, dtype=jnp.float32) * 2.0 / head_size))
    angles = token_positions.astype(jnp.float32)[:, None] * frequency[None, :]
    return (jnp.cos(angles)[:, None, :], jnp.sin(angles)[:, None, :])


def apply_rotation(values, cosine_table, sine_portion):
    half_size = values.shape[-1] // 2
    first_half = values[..., :half_size]
    second = values[..., half_size:]
    return jnp.concatenate(
        [
            first_half * cosine_table - second * sine_portion,
            second * cosine_table + first_half * sine_portion,
        ],
        axis=-1,
    )


def unrotate(grads, cosine_table, sine_portion):
    half_size = grads.shape[-1] // 2
    first_half = grads[..., :half_size]
    second = grads[..., half_size:]
    return jnp.concatenate(
        [
            first_half * cosine_table + second * sine_portion,
            second * cosine_table - first_half * sine_portion,
        ],
        axis=-1,
    )


def normalize_parts(values):
    inverse = lax.rsqrt(jnp.mean(values * values, axis=-1, keepdims=True) + norm_eps)
    return (values * inverse, inverse)


def norm_back(grad_out, scaled, inverse, gain):
    grad_scaled = grad_out * gain
    grad_gain = jnp.sum(grad_out * scaled, axis=0)
    grad_values = inverse * (
        grad_scaled - scaled * jnp.mean(grad_scaled * scaled, axis=-1, keepdims=True)
    )
    return (grad_values, grad_gain)


def padded_columns(columns):
    used = sum(column.shape[1] for column in columns)
    rest = jnp.zeros((columns[0].shape[0], -used % 128), columns[0].dtype)
    return jnp.concatenate([*columns, rest], axis=1)


def shards(
    tokens,
    routes,
    gates,
    qkv_weight,
    out_weight,
    attn_gain,
    moe_gain,
    expert_in,
    expert_out,
    cotangent,
):
    local_row_count = tokens.shape[0]
    width = tokens.shape[1]
    sequence_split_count = lax.axis_size("uly")
    blk_index = lax.axis_index("blk")
    uly_index = lax.axis_index("uly")
    q_heads = QUERY_HEADS // sequence_split_count
    key_value_heads = KEY_VALUE_HEADS // sequence_split_count
    query_group_size = QUERY_HEADS // KEY_VALUE_HEADS
    q_width = q_heads * HEAD_DIMENSION
    kv_width = key_value_heads * HEAD_DIMENSION
    seq_rows = local_row_count * sequence_split_count
    block_size = min(512, seq_rows)
    block_count = seq_rows // block_size
    score_scale = HEAD_DIMENSION ** (-0.5)
    local_experts = E // sequence_split_count
    query_portion = QUERY_HEADS * HEAD_DIMENSION
    key_portion = KEY_VALUE_HEADS * HEAD_DIMENSION
    all_axes = ("dp", "blk", "uly")
    qkv_columns = qkv_weight.shape[1]
    gathered = lax.all_gather(
        jnp.concatenate(
            [qkv_weight, padded_columns([attn_gain[:, None], moe_gain[:, None]])], axis=1
        ),
        all_axes,
        axis=0,
        tiled=True,
    )
    qkv_full = gathered[:, :qkv_columns]
    gain_attn = gathered[:, qkv_columns].astype(jnp.float32)
    gain_moe = gathered[:, qkv_columns + 1].astype(jnp.float32)
    out_full = lax.all_gather(out_weight, all_axes, axis=0, tiled=True)
    slice_count = lax.axis_size("dp") * lax.axis_size("blk")
    hidden_slice = F // slice_count
    hidden_columns = local_experts * hidden_slice
    w_out = expert_out.reshape(hidden_columns, width)
    w_in = lax.all_to_all(
        expert_in.reshape(local_experts, width // slice_count, 2, slice_count, hidden_slice)
        .transpose(3, 1, 2, 0, 4)
        .reshape(slice_count, width // slice_count, 2 * hidden_columns),
        ("dp", "blk"),
        split_axis=0,
        concat_axis=0,
        tiled=True,
    ).reshape(width, 2 * hidden_columns)
    gate_by_expert = jnp.sum(
        jnp.where(
            routes[:, :, None] == jnp.arange(E, dtype=jnp.int32)[None, None, :],
            gates[:, :, None],
            0.0,
        ),
        axis=1,
    )
    gate_high = gate_by_expert.astype(jnp.bfloat16)
    gate_low = (gate_by_expert - gate_high.astype(jnp.float32)).astype(jnp.bfloat16)
    all_cotangent_gates = lax.all_gather(
        jnp.concatenate(
            [cotangent.astype(jnp.bfloat16), padded_columns([gate_high, gate_low])], axis=1
        ),
        all_axes,
        axis=0,
        tiled=True,
    )
    all_cotangent = all_cotangent_gates[:, :width]
    all_gates = all_cotangent_gates[:, width:]
    inputs = tokens.astype(jnp.float32)
    scaled_one, inverse_one = normalize_parts(inputs)
    normed_one = (scaled_one * gain_attn).astype(jnp.bfloat16)
    projected_rows = jnp.dot(normed_one, qkv_full, preferred_element_type=jnp.float32)
    token_positions = (blk_index * sequence_split_count + uly_index) * local_row_count + jnp.arange(
        local_row_count, dtype=jnp.int32
    )
    cosine_table, sine_portion = rope_tables(token_positions, HEAD_DIMENSION)
    queries = apply_rotation(
        projected_rows[:, :query_portion].reshape(local_row_count, QUERY_HEADS, HEAD_DIMENSION),
        cosine_table,
        sine_portion,
    )
    sequence_keys = apply_rotation(
        projected_rows[:, query_portion : query_portion + key_portion].reshape(
            local_row_count, KEY_VALUE_HEADS, HEAD_DIMENSION
        ),
        cosine_table,
        sine_portion,
    )
    sequence_values = projected_rows[:, query_portion + key_portion :]
    packed = jnp.concatenate(
        [
            queries.reshape(local_row_count, sequence_split_count, q_width),
            sequence_keys.reshape(local_row_count, sequence_split_count, kv_width),
            sequence_values.reshape(local_row_count, sequence_split_count, kv_width),
        ],
        axis=2,
    ).astype(jnp.bfloat16)
    by_heads = lax.all_to_all(packed, "uly", split_axis=1, concat_axis=0, tiled=True).reshape(
        seq_rows, q_width + 2 * kv_width
    )
    local_queries = by_heads[:, :q_width]
    kv_own = by_heads[:, q_width:]
    kv_prev = passed_along(kv_own, "blk", 1)
    kv_all = jnp.concatenate([kv_prev, kv_own], axis=0)
    key_rows = kv_all[:, :kv_width].reshape(2 * seq_rows, key_value_heads, HEAD_DIMENSION)
    value_rows = kv_all[:, kv_width:].reshape(2 * seq_rows, key_value_heads, HEAD_DIMENSION)
    query_base = blk_index * seq_rows
    key_positions = (blk_index - 1) * seq_rows + jnp.arange(2 * seq_rows, dtype=jnp.int32)

    def block_scores(first_row):
        query_block = lax.dynamic_slice_in_dim(local_queries, first_row, block_size, 0).reshape(
            block_size, key_value_heads, query_group_size, HEAD_DIMENSION
        )
        scores = (
            jnp.einsum("qkgd,skd->kgqs", query_block, key_rows, preferred_element_type=jnp.float32)
            * score_scale
        )
        query_positions = query_base + first_row + jnp.arange(block_size, dtype=jnp.int32)
        visible = (key_positions[None, :] <= query_positions[:, None]) & (
            key_positions[None, :] >= 0
        )
        return (query_block, jnp.where(visible, scores, masked_score))

    def attend(block_index):
        query_block, scores = block_scores(block_index * block_size)
        row_max = jnp.max(scores, axis=-1, keepdims=True)
        weights = jnp.exp(scores - row_max)
        weight_sum = jnp.sum(weights, axis=-1, keepdims=True)
        probs = (weights / weight_sum).astype(jnp.bfloat16)
        mixed_block = jnp.einsum(
            "kgqs,skd->qkgd", probs, value_rows, preferred_element_type=jnp.float32
        )
        return (
            mixed_block.reshape(block_size, q_width).astype(jnp.bfloat16),
            (row_max + jnp.log(weight_sum))[..., 0],
        )

    head_out, log_sums = lax.map(attend, jnp.arange(block_count, dtype=jnp.int32))
    head_out = head_out.reshape(seq_rows, 1, q_width)
    seq_out = lax.all_to_all(head_out, "uly", split_axis=0, concat_axis=1, tiled=True).reshape(
        local_row_count, query_portion
    )
    attention_out = jnp.dot(seq_out, out_full, preferred_element_type=jnp.float32)
    hidden = inputs + attention_out
    scaled_two, inverse_two = normalize_parts(hidden)
    normed_two = (scaled_two * gain_moe).astype(jnp.bfloat16)
    gate_rows = jnp.arange(all_gates.shape[1], dtype=jnp.int32)
    column_experts = uly_index * local_experts + jnp.repeat(
        jnp.arange(local_experts, dtype=jnp.int32), hidden_slice
    )
    spread = (
        (gate_rows[:, None] < 2 * E) & (lax.rem(gate_rows, E)[:, None] == column_experts[None, :])
    ).astype(jnp.bfloat16)
    gate_table = jnp.dot(all_gates, spread, preferred_element_type=jnp.float32)
    all_rows = lax.all_gather(normed_two, all_axes, axis=0, tiled=True)
    gate_up = jnp.dot(all_rows, w_in, preferred_element_type=jnp.float32)
    gate_part = gate_up[:, :hidden_columns]
    up_part = gate_up[:, hidden_columns:]
    sigmoid_gate = jax.nn.sigmoid(gate_part)
    silu_gate = gate_part * sigmoid_gate
    activated = (silu_gate * up_part * gate_table).astype(jnp.bfloat16)
    mixed_part = jnp.dot(activated, w_out, preferred_element_type=jnp.float32)
    grad_act = (
        jnp.dot(all_cotangent, w_out.T, preferred_element_type=jnp.float32) * gate_table
    )
    grad_gate = grad_act * up_part * sigmoid_gate * (1.0 + gate_part * (1.0 - sigmoid_gate))
    grad_up = grad_act * silu_gate
    grad_gate_up = jnp.concatenate([grad_gate, grad_up], axis=-1).astype(jnp.bfloat16)
    rows_part = jnp.dot(grad_gate_up, w_in.T, preferred_element_type=jnp.float32)
    grad_normed_two = lax.psum_scatter(
        rows_part.astype(jnp.bfloat16), all_axes, scatter_dimension=0, tiled=True
    ).astype(jnp.float32)
    mixed_part, grad_normed_two = lax.optimization_barrier(
        (mixed_part.astype(jnp.bfloat16), grad_normed_two)
    )
    mixed = hidden + lax.psum_scatter(
        mixed_part, all_axes, scatter_dimension=0, tiled=True
    ).astype(jnp.float32)
    grad_w_out = jnp.dot(activated.T, all_cotangent, preferred_element_type=jnp.float32)
    grad_w_in = jnp.dot(all_rows.T, grad_gate_up, preferred_element_type=jnp.float32)
    grad_out_shard = grad_w_out.reshape(local_experts, hidden_slice, width)
    grad_in_shard = (
        lax.all_to_all(
            grad_w_in.astype(jnp.bfloat16).reshape(slice_count, width // slice_count, 2 * hidden_columns),
            ("dp", "blk"),
            split_axis=0,
            concat_axis=0,
            tiled=True,
        )
        .reshape(slice_count, width // slice_count, 2, local_experts, hidden_slice)
        .transpose(3, 1, 2, 0, 4)
        .reshape(local_experts, width // slice_count, 2 * F)
        .astype(jnp.float32)
    )
    grad_hidden_norm, grad_gain_moe = norm_back(grad_normed_two, scaled_two, inverse_two, gain_moe)
    grad_hidden = cotangent + grad_hidden_norm
    hidden_low = grad_hidden.astype(jnp.bfloat16)
    grad_out_weight = jnp.dot(seq_out.T, hidden_low, preferred_element_type=jnp.float32)
    grad_seq_out = jnp.dot(hidden_low, out_full.T, preferred_element_type=jnp.float32).astype(
        jnp.bfloat16
    )
    grad_heads = lax.all_to_all(
        grad_seq_out.reshape(local_row_count, sequence_split_count, q_width),
        "uly",
        split_axis=1,
        concat_axis=0,
        tiled=True,
    ).reshape(seq_rows, q_width)

    def attend_back(carry, block_index):
        grad_keys, grad_values = carry
        first_row = block_index * block_size
        query_block, scores = block_scores(first_row)
        probs = jnp.exp(scores - log_sums[block_index][..., None])
        probs_low = probs.astype(jnp.bfloat16)
        grad_block = lax.dynamic_slice_in_dim(grad_heads, first_row, block_size, 0).reshape(
            block_size, key_value_heads, query_group_size, HEAD_DIMENSION
        )
        grad_values = grad_values + jnp.einsum(
            "kgqs,qkgd->skd", probs_low, grad_block, preferred_element_type=jnp.float32
        )
        grad_probs = jnp.einsum(
            "qkgd,skd->kgqs", grad_block, value_rows, preferred_element_type=jnp.float32
        )
        centre = jnp.sum(probs * grad_probs, axis=-1, keepdims=True)
        grad_scores = (probs * (grad_probs - centre)).astype(jnp.bfloat16)
        grad_query = (
            jnp.einsum("kgqs,skd->qkgd", grad_scores, key_rows, preferred_element_type=jnp.float32)
            * score_scale
        )
        grad_keys = (
            grad_keys
            + jnp.einsum(
                "kgqs,qkgd->skd", grad_scores, query_block, preferred_element_type=jnp.float32
            )
            * score_scale
        )
        return ((grad_keys, grad_values), grad_query.reshape(block_size, q_width))

    zero_kv = jnp.zeros((2 * seq_rows, key_value_heads, HEAD_DIMENSION), jnp.float32)
    (grad_keys, grad_values), grad_queries = lax.scan(
        attend_back, (zero_kv, zero_kv), jnp.arange(block_count, dtype=jnp.int32)
    )
    grad_kv = jnp.concatenate(
        [grad_keys.reshape(2 * seq_rows, kv_width), grad_values.reshape(2 * seq_rows, kv_width)],
        axis=1,
    )
    from_next = passed_along(grad_kv[:seq_rows].astype(jnp.bfloat16), "blk", -1).astype(jnp.float32)
    grad_kv_own = grad_kv[seq_rows:] + from_next
    grad_pack = (
        jnp.concatenate([grad_queries.reshape(seq_rows, q_width), grad_kv_own], axis=1)
        .astype(jnp.bfloat16)
        .reshape(seq_rows, 1, q_width + 2 * kv_width)
    )
    grad_seq = lax.all_to_all(grad_pack, "uly", split_axis=0, concat_axis=1, tiled=True)
    grad_q = unrotate(
        grad_seq[:, :, :q_width]
        .astype(jnp.float32)
        .reshape(local_row_count, QUERY_HEADS, HEAD_DIMENSION),
        cosine_table,
        sine_portion,
    )
    grad_k = unrotate(
        grad_seq[:, :, q_width : q_width + kv_width]
        .astype(jnp.float32)
        .reshape(local_row_count, KEY_VALUE_HEADS, HEAD_DIMENSION),
        cosine_table,
        sine_portion,
    )
    grad_v = (
        grad_seq[:, :, q_width + kv_width :]
        .astype(jnp.float32)
        .reshape(local_row_count, key_portion)
    )
    grad_projected = jnp.concatenate(
        [
            grad_q.reshape(local_row_count, query_portion),
            grad_k.reshape(local_row_count, key_portion),
            grad_v,
        ],
        axis=1,
    ).astype(jnp.bfloat16)
    grad_qkv_weight = jnp.dot(normed_one.T, grad_projected, preferred_element_type=jnp.float32)
    grad_normed_one = jnp.dot(grad_projected, qkv_full.T, preferred_element_type=jnp.float32)
    grad_input_norm, grad_gain_attn = norm_back(grad_normed_one, scaled_one, inverse_one, gain_attn)
    grad_tokens = grad_hidden + grad_input_norm
    out_payload = lax.psum_scatter(
        jnp.concatenate(
            [
                grad_out_weight.astype(jnp.bfloat16),
                padded_columns([grad_gain_moe.astype(jnp.bfloat16)[:, None]]),
            ],
            axis=1,
        ),
        all_axes,
        scatter_dimension=0,
        tiled=True,
    ).astype(jnp.float32)
    qkv_payload = lax.psum_scatter(
        jnp.concatenate(
            [
                grad_qkv_weight.astype(jnp.bfloat16),
                padded_columns([grad_gain_attn.astype(jnp.bfloat16)[:, None]]),
            ],
            axis=1,
        ),
        all_axes,
        scatter_dimension=0,
        tiled=True,
    ).astype(jnp.float32)
    return (
        mixed,
        grad_tokens,
        qkv_payload[:, :qkv_columns],
        out_payload[:, :width],
        qkv_payload[:, qkv_columns],
        out_payload[:, width],
        grad_in_shard,
        grad_out_shard,
    )


def solution(mesh):
    in_specs = (
        P(("dp", "blk", "uly"), None),
        P(("dp", "blk", "uly"), None),
        P(("dp", "blk", "uly"), None),
        P(("dp", "blk", "uly"), None),
        P(("dp", "blk", "uly"), None),
        P(("dp", "blk", "uly")),
        P(("dp", "blk", "uly")),
        P("uly", ("dp", "blk"), None),
        P("uly", ("dp", "blk"), None),
        P(("dp", "blk", "uly"), None),
    )
    out_specs = (
        P(("dp", "blk", "uly"), None),
        P(("dp", "blk", "uly"), None),
        P(("dp", "blk", "uly"), None),
        P(("dp", "blk", "uly"), None),
        P(("dp", "blk", "uly")),
        P(("dp", "blk", "uly")),
        P("uly", ("dp", "blk"), None),
        P("uly", ("dp", "blk"), None),
    )
    return jax.shard_map(shards, mesh=mesh, in_specs=in_specs, out_specs=out_specs, check_vma=False)
```
